32 devices in a mesh: row: 8 (over y, x, core), col: 4 (over z).
Axes of the slice: x: 2, y: 2, z: 4, core: 2. Of those that a mesh axis runs over, the one named last changes fastest.
Arguments:
- counts: int32 [4096, 4096], P('row', 'col'), may hold values from 1 to 5
- sample_weights: float32 [4096, 4096], P('row', 'col'), may hold values from 0.045 to 54
- classes: int32 [4096, 4096], P('row', 'col'), may hold values from 0 to 3
- class_radius: int32 [4], replicated, may hold values from 8 to 64, as said below
Outputs:
- density_first: float32 [4096, 4096], P('row', 'col')
- density_second: float32 [4096, 4096], P('row', 'col')
The draws below stay inside these ranges and needn't reach their ends.
Inputs may be any that keep to these rules, and one draw needn't show every extreme that they name: `class_radius`: the radii rise strictly from class 0 to class 3, and class 3's radius is 64.
All inputs are finite; a program needn't handle non-finite values.
Results may differ from the reference program's by a relative error of at most 0.0001.
Values sent between devices are 32-bit elements; how exact they have to be, the bound alone decides.
A program may use at most 128 MiB of HBM per device.

```python
import math
import jax
import jax.numpy as jnp
from jax import lax

CR = 512
CC = 1024
RMAX = 64
PR = 32
CLASSES = 4
NX = 4096
NY = 4096


def draw_counts(key, part):
    rows = jnp.arange(NX)[:, None]
    columns = jnp.arange(NY)[None, :]
    ceiling = jnp.broadcast_to(2 + 3 * rows // NX + 3 * columns // NY, (NX, NY))
    return jax.random.randint(jax.random.fold_in(key, 3), (NX, NY), 1, ceiling).astype(jnp.int32)


def draw_classes(key, part):
    first_key, second_key = jax.random.split(jax.random.fold_in(key, 7))
    block_rows = max(CR // 2, 1)
    block_columns = max(CC // 2, 1)
    blocks = jax.random.randint(first_key, (NX // block_rows, NY // block_columns), 0, 4)
    spread_grid = jnp.repeat(jnp.repeat(blocks, block_rows, axis=0), block_columns, axis=1)
    bumped = (jax.random.randint(second_key, (NX, NY), 0, 4) == 3).astype(jnp.int32)
    return jnp.minimum(spread_grid + bumped, 3).astype(jnp.int32)


def draw_class_radius(key, part):
    keys = jax.random.split(jax.random.fold_in(key, 11), 3)
    lowest = max(RMAX // 8, 1)
    middle = max(RMAX // 4, lowest)
    first_radius = jax.random.randint(keys[0], (1,), lowest, middle + 1)
    second_radius = jax.random.randint(keys[1], (1,), middle + 1, RMAX // 2 + 1)
    third_radius = jax.random.randint(keys[2], (1,), RMAX // 2 + 1, RMAX)
    widest = jnp.full((1,), RMAX, jnp.int32)
    return jnp.concatenate([first_radius, second_radius, third_radius, widest]).astype(jnp.int32)


def draw_sample_weights(key, part):
    keys = jax.random.split(jax.random.fold_in(key, 5), 3)
    row_scale = jnp.exp(jax.random.uniform(keys[0], (NX, 1), jnp.float32, math.log(0.3), math.log(3.0)))
    column_scale = jnp.exp(jax.random.uniform(keys[1], (1, NY), jnp.float32, math.log(0.3), math.log(3.0)))
    cell_scale = jnp.exp(jax.random.uniform(keys[2], (NX, NY), jnp.float32, math.log(0.5), math.log(2.0)))
    return (row_scale * column_scale * cell_scale).astype(jnp.float32)


def setup_inputs(seed: int = 0) -> dict:
    key_of = jax.random.split(jax.random.key(seed), 5)
    counts = draw_counts(jax.random.fold_in(key_of[4], 71), 0)
    sample_weights = draw_sample_weights(jax.random.fold_in(key_of[4], 71), 0)
    classes = draw_classes(jax.random.fold_in(key_of[4], 71), 0)
    class_radius = draw_class_radius(jax.random.fold_in(key_of[4], 71), 0)
    return dict(counts=counts, sample_weights=sample_weights, classes=classes, class_radius=class_radius)


BACKGROUND = 0.5
HIGHEST_PRECISION = lax.Precision.HIGHEST


def band_pair(radius, reach):
    spread = 0.5 * radius
    offsets = jnp.arange(-reach, reach + 1).astype(jnp.float32)
    inside = (jnp.abs(offsets) <= radius).astype(jnp.float32)
    norm_sum = jnp.sum(jnp.exp(-offsets * offsets / (2.0 * spread * spread)) * inside)
    source = jnp.arange(4 * reach)[:, None]
    target = jnp.arange(2 * reach)[None, :]
    shifts = (source - target - reach).astype(jnp.float32)
    weight = jnp.exp(-shifts * shifts / (2.0 * spread * spread)) * (jnp.abs(shifts) <= radius).astype(jnp.float32) / norm_sum
    return weight[: 2 * reach], weight[2 * reach:]


def along_columns(field, band_upper, band_lower):
    block_width = band_upper.shape[0]
    blocks = field.reshape(field.shape[0], field.shape[1] // block_width, block_width)
    result = jnp.einsum("mjk,ko->mjo", blocks[:, :-1], band_upper, precision=HIGHEST_PRECISION)
    result = result + jnp.einsum("mjk,ko->mjo", blocks[:, 1:], band_lower, precision=HIGHEST_PRECISION)
    return result.reshape(field.shape[0], -1)


def along_rows(field, band_upper, band_lower):
    block_width = band_upper.shape[0]
    blocks = field.reshape(field.shape[0] // block_width, block_width, field.shape[1])
    result = jnp.einsum("jkn,ko->jon", blocks[:-1], band_upper, precision=HIGHEST_PRECISION)
    result = result + jnp.einsum("jkn,ko->jon", blocks[1:], band_lower, precision=HIGHEST_PRECISION)
    return result.reshape(-1, field.shape[1])


def smooth(field, band_upper, band_lower, reach):
    padded = jnp.pad(field, ((0, 0), (reach, reach)))
    partial_field = along_columns(padded, band_upper, band_lower)
    padded = jnp.pad(partial_field, ((reach, reach), (0, 0)))
    return along_rows(padded, band_upper, band_lower)


def reference(counts, sample_weights, classes, class_radius):
    cell_mass = counts.astype(jnp.float32) * sample_weights
    pilot_upper, pilot_lower = band_pair(jnp.float32(PR), PR)
    pilot_field = smooth(cell_mass, pilot_upper, pilot_lower, PR) + BACKGROUND
    mass_sum = jnp.sum(cell_mass)
    radii = class_radius.astype(jnp.float32)
    results = []
    for iteration in range(2):
        mean_log = jnp.sum(cell_mass * jnp.log(pilot_field)) / mass_sum
        adapted = cell_mass * pilot_field / jnp.exp(mean_log)
        density = jnp.zeros_like(adapted)
        for class_index in range(CLASSES):
            band_upper, band_lower = band_pair(radii[class_index], RMAX)
            masked = jnp.where(classes == class_index, adapted, jnp.float32(0.0))
            density = density + smooth(masked, band_upper, band_lower, RMAX)
        results.append(density)
        pilot_field = density + BACKGROUND
    return results[0], results[1]
```

```python
import functools

import jax
import jax.numpy as jnp
from jax import lax
from jax.experimental import pallas as pl
from jax.experimental.pallas import tpu as pltpu
from jax.sharding import PartitionSpec as P

RMAX = 64
PR = 32
BACKGROUND = 0.5
B = 2 * RMAX
K = 2 * B
CHUNK = 16
MESH = pl.DeviceIdType.MESH
F32 = jnp.float32
BF16 = jnp.bfloat16


def split(x):
    high = x.astype(BF16)
    return high, (x - high.astype(F32)).astype(BF16)


def dot(a, b):
    return jnp.dot(a, b, preferred_element_type=F32)


def band(radius, source_dim):
    shape = (K, B) if source_dim == 0 else (B, K)
    source = lax.broadcasted_iota(jnp.int32, shape, source_dim)
    target = lax.broadcasted_iota(jnp.int32, shape, 1 - source_dim)
    spread = 0.5 * radius
    factor = 1.0 / (2.0 * spread * spread)

    def raw(d):
        return jnp.where(jnp.abs(d) <= radius, jnp.exp(-d * d * factor), 0.0)

    offsets = lax.broadcasted_iota(jnp.int32, (8, K), 1) - B
    norm = jnp.sum(raw(offsets.astype(F32))[0:1], axis=1, keepdims=True)
    return raw((source - target - RMAX).astype(F32)) / norm


def kernel(
    rows, cols, classes_n,
    radius_ref, counts_ref, weights_ref, classes_ref,
    first_ref, second_ref,
    mass, field, padded, high, low, mask, swept_h, swept_l,
    row_band, col_band, halo_top, halo_bottom, halo_left, halo_right, corner,
    part, red_row, red_col,
    send_sem, recv_sem, rsend, rrecv, csend, crecv,
):
    r, c = lax.axis_index("row"), lax.axis_index("col")
    tr, tc = counts_ref.shape
    wide = tc + 2 * RMAX
    last = wide - B
    chunks = tr // CHUNK

    steps = [(-1, 0), (1, 0), (0, -1), (0, 1), (-1, -1), (-1, 1), (1, -1), (1, 1)]

    def there(dr, dc):
        ok = jnp.bool_(True)
        if dr < 0:
            ok = ok & (r > 0)
        if dr > 0:
            ok = ok & (r < rows - 1)
        if dc < 0:
            ok = ok & (c > 0)
        if dc > 0:
            ok = ok & (c < cols - 1)
        return ok

    barrier = pltpu.get_barrier_semaphore()
    for d in range(1, rows):
        pl.semaphore_signal(barrier, 1, device_id=(lax.rem(r + d, rows), c), device_id_type=MESH)
    for d in range(1, cols):
        pl.semaphore_signal(barrier, 1, device_id=(r, lax.rem(c + d, cols)), device_id_type=MESH)
    for dr, dc in steps[4:]:
        @pl.when(there(dr, dc))
        def _():
            pl.semaphore_signal(barrier, 1, device_id=(r + dr, c + dc), device_id_type=MESH)
    vertical = (r > 0).astype(jnp.int32) + (r < rows - 1).astype(jnp.int32)
    across = (c > 0).astype(jnp.int32) + (c < cols - 1).astype(jnp.int32)
    pl.semaphore_wait(barrier, rows + cols - 2 + vertical * across)

    def pieces(phase):
        own = padded.at[phase]
        top, bottom = pl.ds(0, RMAX), pl.ds(tr - RMAX, RMAX)
        left, right = pl.ds(0, B), pl.ds(last, B)
        return [
            (own.at[top, :], halo_bottom.at[phase], 1),
            (own.at[bottom, :], halo_top.at[phase], 0),
            (own.at[:, left], halo_right.at[phase], 3),
            (own.at[:, right], halo_left.at[phase], 2),
            (own.at[top, left], corner.at[phase, 3], 7),
            (own.at[top, right], corner.at[phase, 2], 6),
            (own.at[bottom, left], corner.at[phase, 1], 5),
            (own.at[bottom, right], corner.at[phase, 0], 4),
        ]

    def copy_of(phase, n):
        dr, dc = steps[n]
        source, target, slot = pieces(phase)[n]
        return pltpu.make_async_remote_copy(
            src_ref=source, dst_ref=target,
            send_sem=send_sem.at[phase, n], recv_sem=recv_sem.at[phase, slot],
            device_id=(r + dr, c + dc), device_id_type=MESH,
        )

    landing = lambda phase: [
        halo_top.at[phase], halo_bottom.at[phase], halo_left.at[phase], halo_right.at[phase],
        corner.at[phase, 0], corner.at[phase, 1], corner.at[phase, 2], corner.at[phase, 3],
    ]

    def send(phase):
        for n in range(8):
            dr, dc = steps[n]

            @pl.when(there(dr, dc))
            def _():
                copy_of(phase, n).start()

    def clear(phase):
        for n in range(8):
            dr, dc = steps[n]

            @pl.when(jnp.logical_not(there(dr, dc)))
            def _():
                ref = landing(phase)[n]
                ref[...] = jnp.zeros(ref.shape, F32)

    def arrived(phase, which):
        for n in which:
            dr, dc = steps[n]

            @pl.when(there(dr, dc))
            def _():
                ref = landing(phase)[n]
                pltpu.make_async_remote_copy(
                    src_ref=ref, dst_ref=ref, send_sem=send_sem.at[phase, n],
                    recv_sem=recv_sem.at[phase, n],
                    device_id=(r + dr, c + dc), device_id_type=MESH,
                ).wait_recv()

    def sent(phase):
        for n in range(8):
            dr, dc = steps[n]

            @pl.when(there(dr, dc))
            def _():
                copy_of(phase, n).wait_send()

    def shifted(x):
        full = jnp.concatenate([x, jnp.zeros((x.shape[0], 2 * RMAX), F32)], axis=1)
        return pltpu.roll(full, RMAX, axis=1)

    def tile_sum(x):
        total = None
        for a in range(0, x.shape[0], 8):
            for b in range(0, x.shape[1], 128):
                piece = x[a : a + 8, b : b + 128]
                total = piece if total is None else total + piece
        return total

    CLS, PIL, ONE, TWO = 0, 1, 2, 3

    def prepare(i, total):
        at = pl.ds(pl.multiple_of(i * CHUNK, CHUNK), CHUNK)
        inner = pl.ds(pl.multiple_of(i * CHUNK + RMAX, CHUNK), CHUNK)
        m = counts_ref[at, :].astype(F32) * weights_ref[at, :]
        mass[at, :] = m
        s = shifted(m)
        padded[PIL, at, :] = s
        high[inner, :], low[inner, :] = split(s)
        return total + tile_sum(m)

    mass_total = lax.fori_loop(0, chunks, prepare, jnp.zeros((8, 128), F32))
    send(PIL)

    def labels(i, _):
        at = pl.ds(pl.multiple_of(i * CHUNK, CHUNK), CHUNK)
        padded[CLS, at, :] = shifted((classes_ref[at, :] + 1).astype(F32))
        return 0

    lax.fori_loop(0, chunks, labels, 0)
    send(CLS)
    for phase in range(4):
        clear(phase)

    for n in range(classes_n + 1):
        radius = F32(PR) if n == classes_n else radius_ref[n].astype(F32)
        h, l = split(band(radius, 1))
        row_band[n, 0:B, :] = h
        row_band[n, B : 2 * B, :] = l
        h, l = split(band(radius, 0))
        both = jnp.concatenate([h, l], axis=1)
        col_band[n, 0:K, :] = both
        col_band[n, K : 2 * K, :] = both

    def put(at, across, x, masks):
        if masks:
            for n in range(classes_n):
                mask[n, at, across] = jnp.where(x == n + 1.0, 1.0, 0.0).astype(BF16)
        else:
            high[at, across], low[at, across] = split(x)

    inside = pl.ds(B, last - B)

    def rows_in(phase, masks=False):
        def step(i, _):
            at = pl.ds(pl.multiple_of(i * CHUNK, CHUNK), CHUNK)
            below = pl.ds(pl.multiple_of(i * CHUNK + RMAX + tr, CHUNK), CHUNK)
            put(at, inside, halo_top[phase, at, inside], masks)
            put(below, inside, halo_bottom[phase, at, inside], masks)
            return 0

        lax.fori_loop(0, RMAX // CHUNK, step, 0)

    def cols_in(phase, masks=False):
        left, right = pl.ds(0, B), pl.ds(last, B)

        def step(i, _):
            at = pl.ds(pl.multiple_of(i * CHUNK, CHUNK), CHUNK)
            below = pl.ds(pl.multiple_of(i * CHUNK + RMAX + tr, CHUNK), CHUNK)
            put(at, left, halo_top[phase, at, left] + corner[phase, 0, at, :], masks)
            put(at, right, halo_top[phase, at, right] + corner[phase, 1, at, :], masks)
            put(below, left, halo_bottom[phase, at, left] + corner[phase, 2, at, :], masks)
            put(below, right, halo_bottom[phase, at, right] + corner[phase, 3, at, :], masks)
            return 0

        lax.fori_loop(0, RMAX // CHUNK, step, 0)

        def middle(i, _):
            at = pl.ds(pl.multiple_of(i * CHUNK, CHUNK), CHUNK)
            inner = pl.ds(pl.multiple_of(i * CHUNK + RMAX, CHUNK), CHUNK)
            put(inner, left, padded[phase, at, left] + halo_left[phase, at, :], masks)
            put(inner, right, padded[phase, at, right] + halo_right[phase, at, :], masks)
            return 0

        lax.fori_loop(0, chunks, middle, 0)

    def row_piece(i, places, labelled):
        source = pl.ds(pl.multiple_of(i * B, B), K)
        target = pl.ds(pl.multiple_of(i * B, B), B)

        def get(ref, *lead):
            got = [ref[(*lead, source, pl.ds(start, size))] for start, size in places]
            return got[0] if len(got) == 1 else jnp.concatenate(got, axis=1)

        h, l = get(high), get(low)
        for n in range(classes_n) if labelled else (0,):
            if labelled:
                m = get(mask, n)
                xh, xl = h * m, l * m
            else:
                xh, xl = h, l
            w = row_band[n if labelled else classes_n]
            main = dot(w, xh)
            y = main[:B] + main[B:] + dot(w[:B], xl)
            yh, yl = split(y)
            offset = 0
            for start, size in places:
                swept_h[n, target, pl.ds(start, size)] = yh[:, offset : offset + size]
                swept_l[n, target, pl.ds(start, size)] = yl[:, offset : offset + size]
                offset += size

    blocks = tr // B
    pairs = (last - B) // (2 * B)
    odd = (last - B) % (2 * B)

    def row_blocks(indices, labelled):
        low_i, count, stride = indices

        def step(s, _):
            i = low_i + s * stride

            def inner(q, _):
                row_piece(i, [(pl.multiple_of(B + q * 2 * B, B), 2 * B)], labelled)
                return 0

            lax.fori_loop(0, pairs, inner, 0)
            if odd:
                row_piece(i, [(last - odd, odd)], labelled)
            return 0

        lax.fori_loop(0, count, step, 0)

    def edge_blocks(labelled):
        def step(i, _):
            row_piece(i, [(0, B), (last, B)], labelled)
            return 0

        lax.fori_loop(0, blocks, step, 0)

    def col_sweep(target, labelled):
        def step(j, _):
            window = pl.ds(pl.multiple_of(j * B, B), K)
            total = None
            for n in range(classes_n) if labelled else (0,):
                x = jnp.concatenate([swept_h[n, :, window], swept_l[n, :, window]], axis=1)
                term = dot(x, col_band[n if labelled else classes_n])
                total = term if total is None else total + term
            target[:, pl.ds(pl.multiple_of(j * B, B), B)] = total[:, :B] + total[:, B:]
            return 0

        lax.fori_loop(0, tc // B, step, 0)

    def sweep(phase, labelled, between=()):
        between = list(between) + [lambda: None] * 2
        row_blocks((1, blocks - 2, 1), labelled)
        between[0]()
        arrived(phase, (0, 1))
        rows_in(phase)
        row_blocks((0, 2, blocks - 1), labelled)
        between[1]()
        arrived(phase, range(2, 8))
        cols_in(phase)
        edge_blocks(labelled)

    def row_copy(t, d):
        return pltpu.make_async_remote_copy(
            src_ref=part.at[t, 0], dst_ref=red_row.at[t, d],
            send_sem=rsend.at[t, d], recv_sem=rrecv.at[t, d],
            device_id=(lax.rem(r + d, rows), c), device_id_type=MESH,
        )

    def col_copy(t, d):
        return pltpu.make_async_remote_copy(
            src_ref=part.at[t, 1], dst_ref=red_col.at[t, d],
            send_sem=csend.at[t, d], recv_sem=crecv.at[t, d],
            device_id=(r, lax.rem(c + d, cols)), device_id_type=MESH,
        )

    def reduce_start(t, log_total):
        part[t, 0, 0:8, :] = mass_total
        part[t, 0, 8:16, :] = log_total
        for d in range(1, rows):
            row_copy(t, d).start()

    def reduce_middle(t):
        total = part[t, 0]
        for d in range(1, rows):
            row_copy(t, d).wait()
            total = total + red_row[t, d]
        part[t, 1] = total
        for d in range(1, cols):
            col_copy(t, d).start()

    def reduce_end(t):
        total = part[t, 1]
        for d in range(1, cols):
            col_copy(t, d).wait()
            total = total + red_col[t, d]
        mass_sum = jnp.sum(total[0:8], keepdims=True)
        log_sum = jnp.sum(total[8:16], keepdims=True)
        return jnp.exp(-(log_sum / mass_sum))

    def adapt(phase, density_of):
        def step(i, total):
            at = pl.ds(pl.multiple_of(i * CHUNK, CHUNK), CHUNK)
            inner = pl.ds(pl.multiple_of(i * CHUNK + RMAX, CHUNK), CHUNK)
            pilot = density_of(at) + BACKGROUND
            m = mass[at, :]
            s = shifted(m * pilot)
            padded[phase, at, :] = s
            high[inner, :], low[inner, :] = split(s)
            return total + tile_sum(m * jnp.log(pilot))

        total = lax.fori_loop(0, chunks, step, jnp.zeros((8, 128), F32))
        send(phase)
        return total

    sweep(PIL, False)
    col_sweep(field, False)
    log_total = adapt(ONE, lambda at: field[at, :])
    reduce_start(0, log_total)

    def own_masks(i, _):
        at = pl.ds(pl.multiple_of(i * CHUNK, CHUNK), CHUNK)
        inner = pl.ds(pl.multiple_of(i * CHUNK + RMAX, CHUNK), CHUNK)
        put(inner, inside, padded[CLS, at, inside], True)
        return 0

    lax.fori_loop(0, chunks, own_masks, 0)
    arrived(CLS, range(8))
    rows_in(CLS, True)
    cols_in(CLS, True)

    sweep(ONE, True, [lambda: reduce_middle(0)])
    col_sweep(field, True)
    inverse = reduce_end(0)

    def first_density(at):
        density = field[at, :] * inverse
        first_ref[at, :] = density
        return density

    log_total = adapt(TWO, first_density)
    reduce_start(1, log_total)

    sweep(TWO, True, [lambda: reduce_middle(1)])
    col_sweep(field, True)
    inverse_two = reduce_end(1)

    def finish(i, _):
        at = pl.ds(pl.multiple_of(i * CHUNK, CHUNK), CHUNK)
        second_ref[at, :] = field[at, :] * inverse_two
        return 0

    lax.fori_loop(0, chunks, finish, 0)
    for phase in range(4):
        sent(phase)


def body(rows, cols, counts, sample_weights, classes, class_radius):
    tr, tc = counts.shape
    n = class_radius.shape[0]
    wide, tall = tc + 2 * RMAX, tr + 2 * RMAX
    vmem = pl.BlockSpec(memory_space=pltpu.VMEM)
    out = jax.ShapeDtypeStruct((tr, tc), F32)
    return pl.pallas_call(
        functools.partial(kernel, rows, cols, n),
        out_shape=(out, out),
        in_specs=[pl.BlockSpec(memory_space=pltpu.SMEM), vmem, vmem, vmem],
        out_specs=(vmem, vmem),
        scratch_shapes=[
            pltpu.VMEM((tr, tc), F32),
            pltpu.VMEM((tr, tc), F32),
            pltpu.VMEM((4, tr, wide), F32),
            pltpu.VMEM((tall, wide), BF16),
            pltpu.VMEM((tall, wide), BF16),
            pltpu.VMEM((n, tall, wide), BF16),
            pltpu.VMEM((n, tr, wide), BF16),
            pltpu.VMEM((n, tr, wide), BF16),
            pltpu.VMEM((n + 1, 2 * B, K), BF16),
            pltpu.VMEM((n + 1, 2 * K, 2 * B), BF16),
            pltpu.VMEM((4, RMAX, wide), F32),
            pltpu.VMEM((4, RMAX, wide), F32),
            pltpu.VMEM((4, tr, B), F32),
            pltpu.VMEM((4, tr, B), F32),
            pltpu.VMEM((4, 4, RMAX, B), F32),
            pltpu.VMEM((2, 2, 16, 128), F32),
            pltpu.VMEM((2, rows, 16, 128), F32),
            pltpu.VMEM((2, cols, 16, 128), F32),
            pltpu.SemaphoreType.DMA((4, 8)),
            pltpu.SemaphoreType.DMA((4, 8)),
            pltpu.SemaphoreType.DMA((2, rows)),
            pltpu.SemaphoreType.DMA((2, rows)),
            pltpu.SemaphoreType.DMA((2, cols)),
            pltpu.SemaphoreType.DMA((2, cols)),
        ],
        compiler_params=pltpu.CompilerParams(
            collective_id=0, has_side_effects=True, vmem_limit_bytes=60 * 2**20
        ),
    )(class_radius, counts, sample_weights, classes)


def solution(mesh):
    rows, cols = mesh.shape["row"], mesh.shape["col"]
    return jax.shard_map(
        functools.partial(body, rows, cols),
        mesh=mesh,
        in_specs=(P("row", "col"), P("row", "col"), P("row", "col"), P()),
        out_specs=(P("row", "col"), P("row", "col")),
        check_vma=False,
    )
```

```python
import functools

import jax
import jax.numpy as jnp
from jax import lax
from jax.experimental import pallas as pl
from jax.experimental.pallas import tpu as pltpu
from jax.sharding import PartitionSpec as P

RMAX = 64
PR = 32
BACKGROUND = 0.5
B = 2 * RMAX
K = 2 * B
CHUNK = 64
MESH = pl.DeviceIdType.MESH
CLS, PIL, ONE, TWO = 0, 1, 2, 3
F32 = jnp.float32
BF16 = jnp.bfloat16


def split(x):
    high = x.astype(BF16)
    return high, (x - high.astype(F32)).astype(BF16)


def dot(a, b):
    return jnp.dot(a, b, preferred_element_type=F32)


def band(radius, source_dim):
    shape = (K, B) if source_dim == 0 else (B, K)
    source = lax.broadcasted_iota(jnp.int32, shape, source_dim)
    target = lax.broadcasted_iota(jnp.int32, shape, 1 - source_dim)
    spread = 0.5 * radius
    factor = 1.0 / (2.0 * spread * spread)

    def raw(d):
        return jnp.where(jnp.abs(d) <= radius, jnp.exp(-d * d * factor), 0.0)

    offsets = lax.broadcasted_iota(jnp.int32, (8, K), 1) - B
    norm = jnp.sum(raw(offsets.astype(F32))[0:1], axis=1, keepdims=True)
    return raw((source - target - RMAX).astype(F32)) / norm


def kernel(
    rows, cols, classes_n,
    radius_ref, counts_ref, weights_ref, classes_ref,
    first_ref, second_ref, inverse_ref,
    mass, field, padded, packed, high, low, mask, swept_h, swept_l,
    row_band, col_band, halo_top, halo_bottom, halo_left, halo_right, corner,
    part, red_row, red_col,
    send_sem, recv_sem, rsend, rrecv, csend, crecv,
):
    r, c = lax.axis_index("row"), lax.axis_index("col")
    tr, tc = counts_ref.shape
    wide = tc + 2 * RMAX
    last = wide - B
    chunks = tr // CHUNK

    steps = [(-1, 0), (1, 0), (0, -1), (0, 1), (-1, -1), (-1, 1), (1, -1), (1, 1)]

    def there(dr, dc):
        ok = jnp.bool_(True)
        if dr < 0:
            ok = ok & (r > 0)
        if dr > 0:
            ok = ok & (r < rows - 1)
        if dc < 0:
            ok = ok & (c > 0)
        if dc > 0:
            ok = ok & (c < cols - 1)
        return ok

    barrier = pltpu.get_barrier_semaphore()
    for d in range(1, rows):
        pl.semaphore_signal(barrier, 1, device_id=(lax.rem(r + d, rows), c), device_id_type=MESH)
    for d in range(1, cols):
        pl.semaphore_signal(barrier, 1, device_id=(r, lax.rem(c + d, cols)), device_id_type=MESH)
    for dr, dc in steps[4:]:
        @pl.when(there(dr, dc))
        def _():
            pl.semaphore_signal(barrier, 1, device_id=(r + dr, c + dc), device_id_type=MESH)
    vertical = (r > 0).astype(jnp.int32) + (r < rows - 1).astype(jnp.int32)
    across = (c > 0).astype(jnp.int32) + (c < cols - 1).astype(jnp.int32)
    pl.semaphore_wait(barrier, rows + cols - 2 + vertical * across)

    def pieces(phase):
        own = padded.at[phase]
        reach = PR if phase == PIL else RMAX
        top, bottom = pl.ds(0, reach), pl.ds(tr - reach, reach)
        far, near = pl.ds(RMAX - reach, reach), pl.ds(0, reach)
        left, right = pl.ds(0, B), pl.ds(last, B)
        return [
            (own.at[top, :], halo_bottom.at[phase, near], 1),
            (own.at[bottom, :], halo_top.at[phase, far], 0),
            (packed.at[phase, 0], halo_right.at[phase], 3),
            (packed.at[phase, 1], halo_left.at[phase], 2),
            (own.at[top, left], corner.at[phase, 3, near], 7),
            (own.at[top, right], corner.at[phase, 2, near], 6),
            (own.at[bottom, left], corner.at[phase, 1, far], 5),
            (own.at[bottom, right], corner.at[phase, 0, far], 4),
        ]

    def copy_of(phase, n):
        dr, dc = steps[n]
        source, target, slot = pieces(phase)[n]
        return pltpu.make_async_remote_copy(
            src_ref=source, dst_ref=target,
            send_sem=send_sem.at[phase, n], recv_sem=recv_sem.at[phase, slot],
            device_id=(r + dr, c + dc), device_id_type=MESH,
        )

    def landing(phase):
        reach = PR if phase == PIL else RMAX
        far, near = pl.ds(RMAX - reach, reach), pl.ds(0, reach)
        return [
            halo_top.at[phase, far], halo_bottom.at[phase, near],
            halo_left.at[phase], halo_right.at[phase],
            corner.at[phase, 0, far], corner.at[phase, 1, far],
            corner.at[phase, 2, near], corner.at[phase, 3, near],
        ]

    half = tr // 2
    lower = lax.broadcasted_iota(jnp.int32, (half, B), 1) < RMAX

    def pack(phase):
        a = padded[phase, 0:half, 0:B]
        b = padded[phase, half:tr, 0:B]
        packed[phase, 0] = jnp.where(lower, pltpu.roll(b, RMAX, axis=1), a)
        a = padded[phase, 0:half, last : last + B]
        b = padded[phase, half:tr, last : last + B]
        packed[phase, 1] = jnp.where(lower, a, pltpu.roll(b, RMAX, axis=1))

    def send(phase):
        pack(phase)
        for n in range(8):
            dr, dc = steps[n]

            @pl.when(there(dr, dc))
            def _():
                copy_of(phase, n).start()

    def clear(phase):
        for n in range(8):
            dr, dc = steps[n]

            @pl.when(jnp.logical_not(there(dr, dc)))
            def _():
                ref = landing(phase)[n]
                ref[...] = jnp.zeros(ref.shape, F32)

    def arrived(phase, which):
        for n in which:
            dr, dc = steps[n]

            @pl.when(there(dr, dc))
            def _():
                ref = landing(phase)[n]
                pltpu.make_async_remote_copy(
                    src_ref=ref, dst_ref=ref, send_sem=send_sem.at[phase, n],
                    recv_sem=recv_sem.at[phase, n],
                    device_id=(r + dr, c + dc), device_id_type=MESH,
                ).wait_recv()

    def sent(phase):
        for n in range(8):
            dr, dc = steps[n]

            @pl.when(there(dr, dc))
            def _():
                copy_of(phase, n).wait_send()

    def shifted(x):
        full = jnp.concatenate([x, jnp.zeros((x.shape[0], 2 * RMAX), F32)], axis=1)
        return pltpu.roll(full, RMAX, axis=1)

    def tile_sum(x):
        total = None
        for a in range(0, x.shape[0], 8):
            for b in range(0, x.shape[1], 128):
                piece = x[a : a + 8, b : b + 128]
                total = piece if total is None else total + piece
        return total

    def prepare(i, total):
        at = pl.ds(pl.multiple_of(i * CHUNK, CHUNK), CHUNK)
        inner = pl.ds(pl.multiple_of(i * CHUNK + RMAX, CHUNK), CHUNK)
        m = counts_ref[at, :].astype(F32) * weights_ref[at, :]
        mass[at, :] = m
        s = shifted(m)
        padded[PIL, at, :] = s
        high[inner, :], low[inner, :] = split(s)
        return total + tile_sum(m)

    mass_total = lax.fori_loop(0, chunks, prepare, jnp.zeros((8, 128), F32))
    send(PIL)

    def labels(i, _):
        at = pl.ds(pl.multiple_of(i * CHUNK, CHUNK), CHUNK)
        padded[CLS, at, :] = shifted((classes_ref[at, :] + 1).astype(F32))
        return 0

    lax.fori_loop(0, chunks, labels, 0)
    send(CLS)
    for phase in range(4):
        clear(phase)
    if PR < RMAX:
        halo_top[PIL, 0 : RMAX - PR, :] = jnp.zeros((RMAX - PR, wide), F32)
        halo_bottom[PIL, PR:RMAX, :] = jnp.zeros((RMAX - PR, wide), F32)
        corner[PIL, 0:2, 0 : RMAX - PR, :] = jnp.zeros((2, RMAX - PR, B), F32)
        corner[PIL, 2:4, PR:RMAX, :] = jnp.zeros((2, RMAX - PR, B), F32)

    for n in range(classes_n + 1):
        radius = F32(PR) if n == classes_n else radius_ref[n].astype(F32)
        h, l = split(band(radius, 1))
        row_band[n, 0:B, :] = h
        row_band[n, B : 2 * B, :] = l
        h, l = split(band(radius, 0))
        both = jnp.concatenate([h, l], axis=1)
        col_band[n, 0:K, :] = both
        col_band[n, K : 2 * K, :] = both

    def put(at, across, x, masks):
        if masks:
            for n in range(classes_n):
                mask[n, at, across] = jnp.where(x == n + 1.0, 1.0, 0.0).astype(BF16)
        else:
            high[at, across], low[at, across] = split(x)

    inside = pl.ds(B, last - B)

    def rows_in(phase, masks=False):
        def step(i, _):
            at = pl.ds(pl.multiple_of(i * CHUNK, CHUNK), CHUNK)
            below = pl.ds(pl.multiple_of(i * CHUNK + RMAX + tr, CHUNK), CHUNK)
            put(at, inside, halo_top[phase, at, inside], masks)
            put(below, inside, halo_bottom[phase, at, inside], masks)
            return 0

        lax.fori_loop(0, RMAX // CHUNK, step, 0)

    def cols_in(phase, masks=False):
        left, right = pl.ds(0, B), pl.ds(last, B)

        def step(i, _):
            at = pl.ds(pl.multiple_of(i * CHUNK, CHUNK), CHUNK)
            below = pl.ds(pl.multiple_of(i * CHUNK + RMAX + tr, CHUNK), CHUNK)
            put(at, left, halo_top[phase, at, left] + corner[phase, 0, at, :], masks)
            put(at, right, halo_top[phase, at, right] + corner[phase, 1, at, :], masks)
            put(below, left, halo_bottom[phase, at, left] + corner[phase, 2, at, :], masks)
            put(below, right, halo_bottom[phase, at, right] + corner[phase, 3, at, :], masks)
            return 0

        lax.fori_loop(0, RMAX // CHUNK, step, 0)

        low_lanes = lax.broadcasted_iota(jnp.int32, (CHUNK, B), 1) < RMAX

        def middle(i, _):
            at = pl.ds(pl.multiple_of(i * CHUNK, CHUNK), CHUNK)
            under = pl.ds(pl.multiple_of(i * CHUNK + half, CHUNK), CHUNK)
            inner = pl.ds(pl.multiple_of(i * CHUNK + RMAX, CHUNK), CHUNK)
            inner_under = pl.ds(pl.multiple_of(i * CHUNK + half + RMAX, CHUNK), CHUNK)
            x = halo_left[phase, at, :]
            turned = pltpu.roll(x, RMAX, axis=1)
            put(inner, left, jnp.where(low_lanes, x, padded[phase, at, left]), masks)
            put(inner_under, left, jnp.where(low_lanes, turned, padded[phase, under, left]), masks)
            x = halo_right[phase, at, :]
            turned = pltpu.roll(x, RMAX, axis=1)
            put(inner, right, jnp.where(low_lanes, padded[phase, at, right], x), masks)
            put(inner_under, right, jnp.where(low_lanes, padded[phase, under, right], turned), masks)
            return 0

        lax.fori_loop(0, half // CHUNK, middle, 0)

    def row_piece(i, places, labelled):
        source = pl.ds(pl.multiple_of(i * B, B), K)
        target = pl.ds(pl.multiple_of(i * B, B), B)

        def get(ref, *lead):
            got = [ref[(*lead, source, pl.ds(start, size))] for start, size in places]
            return got[0] if len(got) == 1 else jnp.concatenate(got, axis=1)

        h, l = get(high), get(low)
        for n in range(classes_n) if labelled else (0,):
            if labelled:
                m = get(mask, n)
                xh, xl = h * m, l * m
            else:
                xh, xl = h, l
            w = row_band[n if labelled else classes_n]
            main = dot(w, xh)
            y = main[:B] + main[B:] + dot(w[:B], xl)
            yh, yl = split(y)
            offset = 0
            for start, size in places:
                swept_h[n, target, pl.ds(start, size)] = yh[:, offset : offset + size]
                swept_l[n, target, pl.ds(start, size)] = yl[:, offset : offset + size]
                offset += size

    blocks = tr // B
    pairs = (last - B) // (2 * B)
    odd = (last - B) % (2 * B)

    def row_blocks(indices, labelled):
        low_i, count, stride = indices

        def step(s, _):
            i = low_i + s * stride

            def inner(q, _):
                row_piece(i, [(pl.multiple_of(B + q * 2 * B, B), 2 * B)], labelled)
                return 0

            lax.fori_loop(0, pairs, inner, 0)
            if odd:
                row_piece(i, [(last - odd, odd)], labelled)
            return 0

        lax.fori_loop(0, count, step, 0)

    def edge_blocks(labelled):
        def step(i, _):
            row_piece(i, [(0, B), (last, B)], labelled)
            return 0

        lax.fori_loop(0, blocks, step, 0)

    def col_sweep(target, labelled):
        def step(j, _):
            window = pl.ds(pl.multiple_of(j * B, B), K)
            total = None
            for n in range(classes_n) if labelled else (0,):
                x = jnp.concatenate([swept_h[n, :, window], swept_l[n, :, window]], axis=1)
                term = dot(x, col_band[n if labelled else classes_n])
                total = term if total is None else total + term
            target[:, pl.ds(pl.multiple_of(j * B, B), B)] = total[:, :B] + total[:, B:]
            return 0

        lax.fori_loop(0, tc // B, step, 0)

    def sweep(phase, labelled, between=()):
        between = list(between) + [lambda: None] * 2
        row_blocks((1, blocks - 2, 1), labelled)
        between[0]()
        arrived(phase, (0, 1))
        rows_in(phase)
        row_blocks((0, 2, blocks - 1), labelled)
        between[1]()
        arrived(phase, range(2, 8))
        cols_in(phase)
        edge_blocks(labelled)

    def row_copy(t, d):
        return pltpu.make_async_remote_copy(
            src_ref=part.at[t, 0], dst_ref=red_row.at[t, d],
            send_sem=rsend.at[t, d], recv_sem=rrecv.at[t, d],
            device_id=(lax.rem(r + d, rows), c), device_id_type=MESH,
        )

    def col_copy(t, d):
        return pltpu.make_async_remote_copy(
            src_ref=part.at[t, 1], dst_ref=red_col.at[t, d],
            send_sem=csend.at[t, d], recv_sem=crecv.at[t, d],
            device_id=(r, lax.rem(c + d, cols)), device_id_type=MESH,
        )

    def reduce_start(t, log_total):
        part[t, 0, 0:8, :] = mass_total
        part[t, 0, 8:16, :] = log_total
        for d in range(1, rows):
            row_copy(t, d).start()

    def reduce_middle(t):
        total = part[t, 0]
        for d in range(1, rows):
            row_copy(t, d).wait()
            total = total + red_row[t, d]
        part[t, 1] = total
        for d in range(1, cols):
            col_copy(t, d).start()

    def reduce_end(t):
        total = part[t, 1]
        for d in range(1, cols):
            col_copy(t, d).wait()
            total = total + red_col[t, d]
        mass_sum = jnp.sum(total[0:8], keepdims=True)
        log_sum = jnp.sum(total[8:16], keepdims=True)
        return jnp.exp(-(log_sum / mass_sum))

    def adapt(phase, density_of):
        def step(i, total):
            at = pl.ds(pl.multiple_of(i * CHUNK, CHUNK), CHUNK)
            inner = pl.ds(pl.multiple_of(i * CHUNK + RMAX, CHUNK), CHUNK)
            pilot = density_of(at) + BACKGROUND
            m = mass[at, :]
            s = shifted(m * pilot)
            padded[phase, at, :] = s
            high[inner, :], low[inner, :] = split(s)
            return total + tile_sum(m * jnp.log(pilot))

        total = lax.fori_loop(0, chunks, step, jnp.zeros((8, 128), F32))
        send(phase)
        return total

    def own_masks(i, _):
        at = pl.ds(pl.multiple_of(i * CHUNK, CHUNK), CHUNK)
        inner = pl.ds(pl.multiple_of(i * CHUNK + RMAX, CHUNK), CHUNK)
        put(inner, inside, padded[CLS, at, inside], True)
        return 0

    lax.fori_loop(0, chunks, own_masks, 0)
    sweep(PIL, False)
    col_sweep(field, False)
    log_total = adapt(ONE, lambda at: field[at, :])
    reduce_start(0, log_total)

    arrived(CLS, range(8))
    rows_in(CLS, True)
    cols_in(CLS, True)

    sweep(ONE, True, [lambda: None, lambda: reduce_middle(0)])
    col_sweep(first_ref, True)
    inverse = reduce_end(0)
    inverse_ref[0:8, :] = jnp.broadcast_to(inverse, (8, 128))

    def first_density(at):
        return first_ref[at, :] * inverse

    log_total = adapt(TWO, first_density)
    reduce_start(1, log_total)

    sweep(TWO, True, [lambda: None, lambda: reduce_middle(1)])
    col_sweep(second_ref, True)
    inverse_ref[8:16, :] = jnp.broadcast_to(reduce_end(1), (8, 128))
    for phase in range(4):
        sent(phase)


def body(rows, cols, counts, sample_weights, classes, class_radius):
    tr, tc = counts.shape
    n = class_radius.shape[0]
    wide, tall = tc + 2 * RMAX, tr + 2 * RMAX
    vmem = pl.BlockSpec(memory_space=pltpu.VMEM)
    out = jax.ShapeDtypeStruct((tr, tc), F32)
    first, second, inverse = pl.pallas_call(
        functools.partial(kernel, rows, cols, n),
        out_shape=(out, out, jax.ShapeDtypeStruct((16, 128), F32)),
        in_specs=[pl.BlockSpec(memory_space=pltpu.SMEM), vmem, vmem, vmem],
        out_specs=(vmem, vmem, vmem),
        scratch_shapes=[
            pltpu.VMEM((tr, tc), F32),
            pltpu.VMEM((tr, tc), F32),
            pltpu.VMEM((4, tr, wide), F32),
            pltpu.VMEM((4, 2, tr // 2, B), F32),
            pltpu.VMEM((tall, wide), BF16),
            pltpu.VMEM((tall, wide), BF16),
            pltpu.VMEM((n, tall, wide), BF16),
            pltpu.VMEM((n, tr, wide), BF16),
            pltpu.VMEM((n, tr, wide), BF16),
            pltpu.VMEM((n + 1, 2 * B, K), BF16),
            pltpu.VMEM((n + 1, 2 * K, 2 * B), BF16),
            pltpu.VMEM((4, RMAX, wide), F32),
            pltpu.VMEM((4, RMAX, wide), F32),
            pltpu.VMEM((4, tr // 2, B), F32),
            pltpu.VMEM((4, tr // 2, B), F32),
            pltpu.VMEM((4, 4, RMAX, B), F32),
            pltpu.VMEM((2, 2, 16, 128), F32),
            pltpu.VMEM((2, rows, 16, 128), F32),
            pltpu.VMEM((2, cols, 16, 128), F32),
            pltpu.SemaphoreType.DMA((4, 8)),
            pltpu.SemaphoreType.DMA((4, 8)),
            pltpu.SemaphoreType.DMA((2, rows)),
            pltpu.SemaphoreType.DMA((2, rows)),
            pltpu.SemaphoreType.DMA((2, cols)),
            pltpu.SemaphoreType.DMA((2, cols)),
        ],
        compiler_params=pltpu.CompilerParams(
            collective_id=0, has_side_effects=True, vmem_limit_bytes=60 * 2**20
        ),
    )(class_radius, counts, sample_weights, classes)
    return first * inverse[0, 0], second * inverse[8, 0]


def solution(mesh):
    rows, cols = mesh.shape["row"], mesh.shape["col"]
    return jax.shard_map(
        functools.partial(body, rows, cols),
        mesh=mesh,
        in_specs=(P("row", "col"), P("row", "col"), P("row", "col"), P()),
        out_specs=(P("row", "col"), P("row", "col")),
        check_vma=False,
    )
```
